32 devices in a mesh: replica: 8 (over z, x), shard: 4 (over y, core).
Axes of the slice: x: 2, y: 2, z: 4, core: 2. Of those that a mesh axis runs over, the one named last changes fastest.
Arguments:
- tokens: bfloat16 [32, 1024, 768], P(('replica', 'shard')), may hold values from -6 to 6
- segments: int32 [32, 1024], P(('replica', 'shard')), may hold values from 0 to 3, never falling along the last dimension, each value on 1 to 512 neighbouring positions
- out_grad: bfloat16 [32, 1024, 768], P(('replica', 'shard')), may hold values from -6 to 6
- ln1_gain: bfloat16 [768], P('shard'), may hold values from 0.5 to 1.5
- ln1_bias: bfloat16 [768], P('shard'), may hold values from -2 to 2
- w_qkv: bfloat16 [768, 2304], P('shard'), may hold values from -0.3125 to 0.3125
- b_qkv: bfloat16 [2304], P('shard'), may hold values from -2 to 2
- w_attn: bfloat16 [768, 768], P('shard'), may hold values from -0.625 to 0.625
- b_attn: bfloat16 [768], P('shard'), may hold values from -2 to 2
- ln2_gain: bfloat16 [768], P('shard'), may hold values from 0.5 to 1.5
- ln2_bias: bfloat16 [768], P('shard'), may hold values from -2 to 2
- w_up: bfloat16 [768, 3072], P('shard'), may hold values from -0.21875 to 0.21875
- b_up: bfloat16 [3072], P('shard'), may hold values from -2 to 2
- w_down: bfloat16 [3072, 768], P('shard'), may hold values from -0.109375 to 0.109375
- b_down: bfloat16 [768], P('shard'), may hold values from -2 to 2
Outputs:
- mixed: float32 [32, 1024, 768], P(('replica', 'shard'))
- tokens_grad: float32 [32, 1024, 768], P(('replica', 'shard'))
- grad_ln1_gain: float32 [768], P('shard')
- grad_ln1_bias: float32 [768], P('shard')
- grad_w_qkv: float32 [768, 2304], P('shard')
- grad_b_qkv: float32 [2304], P('shard')
- grad_w_attn: float32 [768, 768], P('shard')
- grad_b_attn: float32 [768], P('shard')
- grad_ln2_gain: float32 [768], P('shard')
- grad_ln2_bias: float32 [768], P('shard')
- grad_w_up: float32 [768, 3072], P('shard')
- grad_b_up: float32 [3072], P('shard')
- grad_w_down: float32 [3072, 768], P('shard')
- grad_b_down: float32 [768], P('shard')
The draws below stay inside these ranges and needn't reach their ends.
Inputs may be any that keep to these rules, and one draw needn't show every extreme that they name: `segments`: within each sequence the numbers never fall; each document spans 1 to 512 tokens, one of them exactly 512.
All inputs are finite; a program needn't handle non-finite values.
Results may differ from the reference program's by a relative error of at most 0.012.
The reference program's roundings to bfloat16 on the way count: a program that leaves them out, or rounds other values in their place, can miss the bound.
Values may be sent and summed in bfloat16 or wider, within the bound.
A program may use at most 320 MiB of HBM per device.

```python
import math
import jax
import jax.numpy as jnp
import numpy as np
from jax import lax

D = 768
HEADS = 12
HEAD = 64
FF = 3072
ROT = 16
LEN = 1024
SEQS = 32


def block_scale(key, shape, cuts, smallest, high):
    loudness, own = 1.0, jax.random.fold_in(key, 6)
    for dim, blocks in cuts:
        heights = jnp.exp(jax.random.uniform(jax.random.fold_in(own, dim), (blocks,), jnp.float32, smallest / len(cuts), high / len(cuts)))
        loudness = loudness * jnp.repeat(heights, shape[dim] // blocks).reshape([-1 if axis == dim else 1 for axis in range(len(shape))])
    return loudness


def profile(count, total, reach, slope):
    weights = [(1 << 20) // math.isqrt(rank ** slope) + 1 for rank in range(2, count + 1)]
    rest, given = total - reach - (count - 1), [1] * (count - 1)
    while rest > 0:
        free = [i for i in range(count - 1) if given[i] < reach]
        pool, left = sum([weights[i] for i in free]), rest
        for i in free:
            more = min(reach - given[i], max(1, left * weights[i] // pool), rest)
            given[i] = given[i] + more
            rest = rest - more
    return np.array([reach] + given)


def ragged_sizes(rng, number_of, total, bound, lean):
    if number_of == 2:
        one = jax.random.randint(rng, (), max(1, total - bound), min(bound, total - 1) + 1)
        return jnp.stack([one, total - one])
    tallies = jnp.asarray(profile(number_of, total, bound, lean), jnp.int32)
    pairs = (number_of - 1) // 2
    giver, taker = tallies[1:1 + 2 * pairs:2], tallies[2:2 + 2 * pairs:2]
    room = jnp.minimum(giver - 1, bound - taker)
    moved = jax.random.randint(jax.random.fold_in(rng, 1), (pairs,), 0, 1 << 20) % (room + 1)
    tallies = tallies.at[1:1 + 2 * pairs:2].set(giver - moved).at[2:2 + 2 * pairs:2].set(taker + moved)
    return tallies[jax.random.permutation(jax.random.fold_in(rng, 2), number_of)]


def centred(own_key, dims, deviation, most, shards=(), kind=jnp.bfloat16):
    drawn = deviation * jax.random.normal(own_key, dims, jnp.float32)
    if shards:
        drawn = drawn * block_scale(own_key, dims, shards, -0.22, 0.18)
    return jnp.clip(drawn, -most, most).astype(kind)


def setup_inputs(seed: int = 0) -> dict:
    key_of = jax.random.split(jax.random.key(seed), 16)
    return {
        "tokens": centred(key_of[0], (SEQS, LEN, D), 1.0, 6.0, ((0, 32),)),
        "segments": jax.vmap(lambda own: jnp.searchsorted(jnp.cumsum(ragged_sizes(own, 4, LEN, LEN // 2, 0)), jnp.arange(LEN), side="right"))(jax.random.split(key_of[1], SEQS)).reshape((SEQS, LEN)).astype(jnp.int32),
        "out_grad": centred(key_of[2], (SEQS, LEN, D), 1.0, 6.0, ((0, 32),)),
        "ln1_gain": jnp.clip(1.0 + 0.1 * jax.random.normal(key_of[3], (D,), jnp.float32), 0.5, 1.5).astype(jnp.bfloat16),
        "ln1_bias": centred(key_of[4], (D,), 0.3, 2.0, ((0, 4),)),
        "w_qkv": centred(key_of[5], (D, 3 * D), (D // 2) ** -0.5, 0.3125, ((0, 4),)),
        "b_qkv": centred(key_of[6], (3 * D,), 0.3, 2.0, ((0, 4),)),
        "w_attn": centred(key_of[7], (D, D), (D // 8) ** -0.5, 0.625, ((0, 4),)),
        "b_attn": centred(key_of[8], (D,), 0.3, 2.0, ((0, 4),)),
        "ln2_gain": jnp.clip(1.0 + 0.1 * jax.random.normal(key_of[9], (D,), jnp.float32), 0.5, 1.5).astype(jnp.bfloat16),
        "ln2_bias": centred(key_of[10], (D,), 0.3, 2.0, ((0, 4),)),
        "w_up": centred(key_of[11], (D, FF), D ** -0.5, 0.21875, ((0, 4),)),
        "b_up": centred(key_of[12], (FF,), 0.3, 2.0, ((0, 4),)),
        "w_down": centred(key_of[13], (FF, D), FF ** -0.5, 0.109375, ((0, 4),)),
        "b_down": centred(key_of[14], (D,), 0.3, 2.0, ((0, 4),)),
    }


EPS = 1e-05
MASKED = -1e+30
ROTARY_BASE = 10000.0

@jax.custom_vjp
def low(v):
    return lax.optimization_barrier(v.astype(jnp.bfloat16)).astype(jnp.float32)

@jax.custom_vjp
def low_back(v):
    return v

def low_keep(v):
    return (low(v), None)

def low_pass(kept, grad):
    return (grad,)

def back_keep(v):
    return (v, None)

def back_low(kept, grad):
    return (low(grad),)
low.defvjp(low_keep, low_pass)
low_back.defvjp(back_keep, back_low)

def both_ways(value):
    return low(low_back(value))

def layer_norm(inputs, gain, bias):
    average = lax.optimization_barrier(jnp.mean(inputs, -1, keepdims=True))
    centered = inputs - average
    variance = lax.optimization_barrier(jnp.mean(centered * centered, -1, keepdims=True))
    inv_scale = lax.rsqrt(variance + EPS)
    normal = centered * inv_scale
    return normal * gain + bias

def positions(segments):
    position_index = lax.broadcasted_iota(jnp.int32, segments.shape, segments.ndim - 1)
    first_flag = jnp.ones(segments.shape[:-1] + (1,), jnp.bool_)
    change = jnp.concatenate([first_flag, segments[..., 1:] != segments[..., :-1]], -1)
    doc_start = lax.cummax(jnp.where(change, position_index, 0), axis=segments.ndim - 1)
    return (position_index - doc_start).astype(jnp.int32)

def rotary_tables(places):
    half_width = ROT // 2
    frequency = ROTARY_BASE ** (-(jnp.arange(half_width, dtype=jnp.float32) * 2.0 / ROT))
    angles = places.astype(jnp.float32)[..., None] * frequency
    cosine = jnp.cos(angles)
    sine_table = jnp.sin(angles)
    return (jnp.concatenate([cosine, cosine], -1), jnp.concatenate([sine_table, sine_table], -1))

def rotate(field, cosine, sine_table):
    rotary_width = cosine.shape[-1]
    half_width = rotary_width // 2
    rotated_part = field[..., :rotary_width]
    turned = jnp.concatenate([-rotated_part[..., half_width:], rotated_part[..., :half_width]], -1)
    return jnp.concatenate([rotated_part * cosine + turned * sine_table, field[..., rotary_width:]], -1)

def forward_sequence(inputs, parameters, cosine, sine_table, allowed):
    ln1_gain, ln1_bias, w_qkv, b_qkv, w_attn, b_attn, ln2_gain, ln2_bias, w_up, b_up, w_down, b_down = parameters
    highest = lax.Precision.HIGHEST
    length = inputs.shape[0]
    normed_one = low(layer_norm(inputs, ln1_gain, ln1_bias))
    mixed_qkv = low_back(jnp.dot(normed_one, w_qkv, precision=highest) + b_qkv)
    qkv_parts = mixed_qkv.reshape(length, 3, HEADS, HEAD)
    queries = low(rotate(qkv_parts[:, 0], cosine, sine_table))
    key_rows = low(rotate(qkv_parts[:, 1], cosine, sine_table))
    value_rows = low(qkv_parts[:, 2])
    scores = low_back(jnp.einsum('qhd,khd->hqk', queries, key_rows, precision=highest) * HEAD ** (-0.5))
    scores = jnp.where(allowed[None], scores, MASKED)
    probabilities = low(jax.nn.softmax(scores, axis=-1))
    context = both_ways(jnp.einsum('hqk,khd->qhd', probabilities, value_rows, precision=highest).reshape(length, D))
    attn_out = jnp.dot(context, w_attn, precision=highest) + b_attn
    normed_two = low(layer_norm(inputs, ln2_gain, ln2_bias))
    hidden = low_back(jnp.dot(normed_two, w_up, precision=highest) + b_up)
    activated = low(jax.nn.gelu(hidden, approximate=False))
    mlp_out = jnp.dot(activated, w_down, precision=highest) + b_down
    return inputs + attn_out + mlp_out

def reference(tokens, segments, out_grad, ln1_gain, ln1_bias, w_qkv, b_qkv, w_attn, b_attn, ln2_gain, ln2_bias, w_up, b_up, w_down, b_down):
    weights_in = (ln1_gain, ln1_bias, w_qkv, b_qkv, w_attn, b_attn, ln2_gain, ln2_bias, w_up, b_up, w_down, b_down)
    parameters = tuple((member.astype(jnp.float32) for member in weights_in))
    places = positions(segments)
    cosine_all, sine_all = rotary_tables(places)
    length = segments.shape[1]
    position_index = jnp.arange(length, dtype=jnp.int32)
    causal = position_index[:, None] >= position_index[None, :]

    def sequence_step(summed, seq_items):
        inputs, seg_seq, cosine, sine_table, cotangent = seq_items
        allowed = causal & (seg_seq[:, None] == seg_seq[None, :])

        def forward_fn(inputs_f, *weights_f):
            return forward_sequence(inputs_f, weights_f, cosine[:, None, :], sine_table[:, None, :], allowed)
        mixed, pullback = jax.vjp(forward_fn, inputs.astype(jnp.float32), *parameters)
        pulled = pullback(cotangent.astype(jnp.float32))
        summed = jax.tree.map(jnp.add, summed, tuple(pulled[1:]))
        return (summed, (mixed, pulled[0]))
    initial = tuple((jnp.zeros_like(member) for member in parameters))
    summed, (mixed_all, grad_all) = lax.scan(sequence_step, initial, (tokens, segments, cosine_all, sine_all, out_grad))
    return (mixed_all, grad_all, summed[0], summed[1], summed[2], summed[3], summed[4], summed[5], summed[6], summed[7], summed[8], summed[9], summed[10], summed[11])
```

```python
import functools
import math

import jax
import jax.numpy as jnp
from jax import lax
from jax.experimental import pallas as pl
from jax.experimental.pallas import tpu as pltpu
from jax.sharding import PartitionSpec as P

HEADS = 12
HEAD = 64
ROT = 16
PAIR = 2 * HEAD
SPAN = 512
BLOCK = 256

EPS = 1e-05
MASKED = -1e30
ROTARY_BASE = 10000.0

f32 = jnp.float32
bf16 = jnp.bfloat16


def swap(value, axis, size, bit):
    return lax.ppermute(value, axis, [(i, i ^ bit) for i in range(size)])


def bits_of(size):
    bits = []
    bit = 1
    while bit < size:
        bits.append(bit)
        bit *= 2
    return bits


def take(blocks, index):
    return lax.dynamic_index_in_dim(blocks, index, 0, keepdims=False)


def gather_rows(rows, shards):
    me = lax.axis_index("shard")
    blocks = rows[None]
    for bit in reversed(bits_of(shards)):
        other = swap(blocks, "shard", shards, bit)
        high = (me // bit) % 2 == 1
        first = jnp.where(high, other, blocks)
        second = jnp.where(high, blocks, other)
        blocks = jnp.stack([first, second], 0)
        blocks = blocks.reshape((-1,) + rows.shape) if bit == shards // 2 else blocks
        if bit != shards // 2:
            blocks = jnp.swapaxes(blocks, 0, 1).reshape((-1,) + rows.shape)
    return blocks.reshape((shards * rows.shape[0],) + rows.shape[1:])


def reduce_rows(grad, shards, replicas):
    me = lax.axis_index("shard")
    rep = lax.axis_index("replica")
    width = grad.shape[1]
    blocks = grad.astype(bf16).reshape(shards, -1, width)
    for bit in bits_of(shards):
        mine = (me // bit) % 2
        pairs = blocks.reshape((-1, 2) + blocks.shape[1:])
        kept = lax.dynamic_index_in_dim(pairs, mine, 1, keepdims=False)
        sent = lax.dynamic_index_in_dim(pairs, 1 - mine, 1, keepdims=False)
        other = swap(sent, "shard", shards, bit)
        blocks = (kept.astype(f32) + other.astype(f32)).astype(bf16)
    part = blocks[0]
    for bit in bits_of(replicas):
        mine = (rep // bit) % 2
        halves = part.reshape(2, -1, width)
        other = swap(take(halves, 1 - mine), "replica", replicas, bit)
        part = (take(halves, mine).astype(f32) + other.astype(f32)).astype(bf16)
    for bit in reversed(bits_of(replicas)):
        high = (rep // bit) % 2 == 1
        other = swap(part, "replica", replicas, bit)
        part = jnp.concatenate(
            [jnp.where(high, other, part), jnp.where(high, part, other)], 0
        )
    return part.astype(f32)


def total_vectors(vectors, shards, replicas):
    me = lax.axis_index("shard")
    packed = jnp.concatenate(vectors)[None]
    for bit in bits_of(shards):
        packed = packed + swap(packed, "shard", shards, bit)
    for bit in bits_of(replicas):
        packed = packed + swap(packed, "replica", replicas, bit)
    owned = []
    offset = 0
    for vector in vectors:
        size = vector.shape[0] // shards
        owned.append(lax.dynamic_slice(packed[0], (offset + me * size,), (size,)))
        offset += vector.shape[0]
    return owned


def dot(a, b, a_dim, b_dim):
    return lax.dot_general(a, b, (((a_dim,), (b_dim,)), ((), ())), preferred_element_type=f32)


def attention_kernel(
    q_ref, k_ref, v_ref, g_ref, cos_ref, low_ref, high_ref, start_ref,
    ctx_ref, dq_ref, dk_ref, dv_ref,
    q_s, k_s, v_s, dk_s, dv_s,
):
    length = q_ref.shape[0]
    cosine, low, high = cos_ref[...], low_ref[...], high_ref[...]

    def turned(u):
        return u * cosine + pltpu.roll(u, PAIR - ROT // 2, 1) * low + pltpu.roll(u, ROT // 2, 1) * high

    def back(rows, d):
        c, lo, hi = cos_ref[rows, :], low_ref[rows, :], high_ref[rows, :]
        return d * c - pltpu.roll(d, PAIR - ROT // 2, 1) * lo - pltpu.roll(d, ROT // 2, 1) * hi

    lane = lax.broadcasted_iota(jnp.int32, (1, PAIR), 1)
    heads = [lane < HEAD, lane >= HEAD]
    q_s[...] = (turned(q_ref[...]).astype(bf16).astype(f32) * HEAD ** (-0.5)).astype(bf16)
    k_s[...] = turned(k_ref[...]).astype(bf16)
    v_s[...] = v_ref[...].astype(bf16)
    dk_s[...] = jnp.zeros_like(dk_s)
    dv_s[...] = jnp.zeros_like(dv_s)

    def only(value, head):
        return jnp.where(head, value, jnp.zeros_like(value))

    for q0 in range(0, length, BLOCK):
        k0 = max(0, q0 - SPAN)
        count = q0 + BLOCK - k0
        rows = pl.ds(q0, BLOCK)
        keys = pl.ds(k0, count)
        q_block, g_block = q_s[rows, :], g_ref[rows, :]
        k_band, v_band = k_s[keys, :], v_s[keys, :]
        key_index = k0 + lax.broadcasted_iota(jnp.int32, (count, BLOCK), 0)
        query_index = q0 + lax.broadcasted_iota(jnp.int32, (count, BLOCK), 1)
        allowed = (key_index >= start_ref[:, rows]) & (key_index <= query_index)
        context = None
        for head in heads:
            q_head, g_head = only(q_block, head), only(g_block, head)
            scores = jnp.where(allowed, dot(k_band, q_head, 1, 1), MASKED)
            exponent = jnp.exp(scores - jnp.max(scores, 0, keepdims=True))
            probs = exponent * (1.0 / jnp.sum(exponent, 0, keepdims=True))
            probs_low = probs.astype(bf16)
            grad_probs = dot(v_band, g_head, 1, 1)
            product = probs * grad_probs
            inner = jnp.sum(product, 0, keepdims=True)
            grad_scores = (product - probs * inner).astype(bf16)
            ctx_part = dot(probs_low, only(v_band, head), 0, 0)
            dq_part = dot(grad_scores, only(k_band, head), 0, 0)
            context = ctx_part if context is None else context + ctx_part
            grad_q = dq_part if head is heads[0] else grad_q + dq_part
            dv_s[keys, :] += dot(probs_low, g_head, 1, 0)
            dk_s[keys, :] += dot(grad_scores, q_head, 1, 0)
        ctx_ref[rows, :] = context.astype(bf16)
        dq_ref[rows, :] = back(rows, grad_q * HEAD ** (-0.5)).astype(bf16)
    dk_ref[...] = back(slice(None), dk_s[...]).astype(bf16)
    dv_ref[...] = dv_s[...].astype(bf16)


def attention(qkv, grad_context, cosine, low, high, start):
    length, width = grad_context.shape
    pairs = width // PAIR
    block = lambda shift: pl.BlockSpec((length, PAIR), lambda i: (0, i + shift))
    table = pl.BlockSpec((length, PAIR), lambda i: (0, 0))
    out = jax.ShapeDtypeStruct((length, width), bf16)
    return pl.pallas_call(
        attention_kernel,
        grid=(pairs,),
        in_specs=[
            block(0), block(pairs), block(2 * pairs), block(0), table, table, table,
            pl.BlockSpec((1, length), lambda i: (0, 0)),
        ],
        out_specs=[block(0)] * 4,
        out_shape=[out] * 4,
        scratch_shapes=[pltpu.VMEM((length, PAIR), bf16)] * 3
        + [pltpu.VMEM((length, PAIR), f32)] * 2,
        compiler_params=pltpu.CompilerParams(vmem_limit_bytes=48 * 1024 * 1024),
        cost_estimate=pl.CostEstimate(
            flops=60_000_000_000, bytes_accessed=20_000_000, transcendentals=8_000_000
        ),
    )(qkv, qkv, qkv, grad_context, cosine, low, high, start)


def norm_back(cotangent, normal, inv_scale, gain):
    scaled = cotangent * gain
    first_term = jnp.mean(scaled, -1, keepdims=True)
    second_term = jnp.mean(scaled * normal, -1, keepdims=True)
    return inv_scale * (scaled - first_term - normal * second_term)


def rotary_tables(places):
    half = ROT // 2
    frequency = ROTARY_BASE ** (-(jnp.arange(half, dtype=f32) * 2.0 / ROT))
    angles = places.astype(f32)[:, None] * jnp.tile(frequency, PAIR // half)[None]
    lane = lax.broadcasted_iota(jnp.int32, angles.shape, 1) % HEAD
    sine = jnp.sin(angles)
    cosine = jnp.where(lane < ROT, jnp.cos(angles), 1.0)
    low = jnp.where(lane < half, -sine, 0.0)
    high = jnp.where((lane >= half) & (lane < ROT), sine, 0.0)
    return cosine, low, high


def matmul(a, b):
    return jnp.dot(a, b, preferred_element_type=f32)


def per_device(
    shards, replicas,
    tokens, segments, out_grad,
    ln1_gain, ln1_bias, w_qkv, b_qkv, w_attn, b_attn,
    ln2_gain, ln2_bias, w_up, b_up, w_down, b_down,
):
    _, length, width = tokens.shape
    vectors = [ln1_gain, ln1_bias, b_qkv, b_attn, ln2_gain, ln2_bias, b_up, b_down]
    packed = gather_rows(jnp.concatenate(vectors)[None], shards)
    full = []
    offset = 0
    for vector in vectors:
        size = vector.shape[0]
        full.append(packed[:, offset : offset + size].reshape(-1).astype(f32))
        offset += size
    gain_one, bias_one, bias_qkv, bias_attn, gain_two, bias_two, bias_up, bias_down = full
    full_up = gather_rows(w_up, shards)
    full_down = gather_rows(w_down, shards)
    full_qkv = gather_rows(w_qkv, shards)
    full_attn = gather_rows(w_attn, shards)

    grad_rows = out_grad.reshape(length, width)
    grad_float = grad_rows.astype(f32)
    inputs = tokens.reshape(length, width).astype(f32)
    centered = inputs - jnp.mean(inputs, -1, keepdims=True)
    inv_scale = lax.rsqrt(jnp.mean(centered * centered, -1, keepdims=True) + EPS)
    normal = centered * inv_scale
    normed_one = (normal * gain_one + bias_one).astype(bf16)
    normed_two = (normal * gain_two + bias_two).astype(bf16)

    hidden = matmul(normed_two, full_up) + bias_up
    cdf = 0.5 * (1.0 + lax.erf(hidden * (1.0 / math.sqrt(2.0))))
    activated = (hidden * cdf).astype(bf16)
    grad_w_down = dot(activated, grad_rows, 0, 0)
    out_down = reduce_rows(grad_w_down, shards, replicas)
    density = jnp.exp(-0.5 * hidden * hidden) * (1.0 / math.sqrt(2.0 * math.pi))
    slope = cdf + hidden * density
    grad_hidden = (dot(grad_rows, full_down, 1, 1) * slope).astype(bf16)
    grad_w_up = dot(normed_two, grad_hidden, 0, 0)
    out_up = reduce_rows(grad_w_up, shards, replicas)
    mlp_out = matmul(activated, full_down) + bias_down
    grad_normed_two = dot(grad_hidden, full_up, 1, 1)

    seg = segments.reshape(length)
    start = jnp.sum((seg[None, :] < seg[:, None]).astype(jnp.int32), 1)
    places = lax.iota(jnp.int32, length) - start
    cosine, low, high = rotary_tables(places)
    qkv = matmul(normed_one, full_qkv) + bias_qkv
    grad_context = dot(grad_rows, full_attn, 1, 1).astype(bf16)
    context, dq, dk, dv = attention(qkv, grad_context, cosine, low, high, start[None])
    grad_qkv = jnp.concatenate([dq, dk, dv], 1)
    grad_w_qkv = dot(normed_one, grad_qkv, 0, 0)
    out_qkv = reduce_rows(grad_w_qkv, shards, replicas)
    grad_w_attn = dot(context, grad_rows, 0, 0)
    out_attn = reduce_rows(grad_w_attn, shards, replicas)
    grad_normed_one = dot(grad_qkv, full_qkv, 1, 1)

    mixed = inputs + (matmul(context, full_attn) + bias_attn) + mlp_out
    tokens_grad = (
        grad_float
        + norm_back(grad_normed_one, normal, inv_scale, gain_one)
        + norm_back(grad_normed_two, normal, inv_scale, gain_two)
    )
    sums = total_vectors(
        [
            jnp.sum(grad_normed_one * normal, 0),
            jnp.sum(grad_normed_one, 0),
            jnp.sum(grad_qkv.astype(f32), 0),
            jnp.sum(grad_float, 0),
            jnp.sum(grad_normed_two * normal, 0),
            jnp.sum(grad_normed_two, 0),
            jnp.sum(grad_hidden.astype(f32), 0),
        ],
        shards,
        replicas,
    )
    g_gain_one, g_bias_one, g_b_qkv, g_b_attn, g_gain_two, g_bias_two, g_b_up = sums
    return (
        mixed[None], tokens_grad[None],
        g_gain_one, g_bias_one, out_qkv, g_b_qkv, out_attn, g_b_attn,
        g_gain_two, g_bias_two, out_up, g_b_up, out_down, g_b_attn,
    )


def solution(mesh):
    rows = P(("replica", "shard"), None, None)
    vec = P("shard")
    mat = P("shard", None)
    in_specs = (
        rows, P(("replica", "shard"), None), rows,
        vec, vec, mat, vec, mat, vec, vec, vec, mat, vec, mat, vec,
    )
    out_specs = (rows, rows, vec, vec, mat, vec, mat, vec, vec, vec, mat, vec, mat, vec)
    body = functools.partial(per_device, mesh.shape["shard"], mesh.shape["replica"])
    return jax.shard_map(body, mesh=mesh, in_specs=in_specs, out_specs=out_specs, check_vma=False)
```
